256 devices in a mesh: section: 2 (over core), ep: 32 (over x, z), tp: 4 (over y).
Axes of the slice: x: 4, y: 4, z: 8, core: 2. Of those that a mesh axis runs over, the one named last changes fastest.
Arguments:
- out_grad: bfloat16 [2, 4096, 7168], P('section', 'ep', 'tp'), may hold values from -6 to 6
- expert_ids: int32 [2, 4096, 8], P('section', 'ep'), may hold values from 0 to 31, all different within a row; in each aligned block of 128 rows (0 to 127, 128 to 255, ..., all dimensions but the last counted through in order) at most 40 rows name the same one
- gates: float32 [2, 4096, 8], P('section', 'ep'), may hold values from 0.05 to 0.6
- w_gate: bfloat16 [2, 32, 7168, 1024], P('section', 'ep', 'tp'), may hold values from -0.0625 to 0.0625
- w_up: bfloat16 [2, 32, 7168, 1024], P('section', 'ep', 'tp'), may hold values from -0.0625 to 0.0625
- w_down: bfloat16 [2, 32, 1024, 7168], P('section', 'ep', None, 'tp'), may hold values from -0.1875 to 0.1875
- gate_saved: bfloat16 [2, 32, 1024, 1280], P('section', 'ep', 'tp'), may hold values from -4 to 4
- up_saved: bfloat16 [2, 32, 1024, 1280], P('section', 'ep', 'tp'), may hold values from -4 to 4
Outputs:
- handed_grad: bfloat16 [2, 4096, 7168], P('section', 'ep', 'tp')
The draws below stay inside these ranges and needn't reach their ends.
Inputs may be any that keep to these rules, and one draw needn't show every extreme that they name: `expert_ids`: each row names 8 different experts; within one section, the rows of one index of ep name any expert at most 40 times, a bound that some block reaches.
All inputs are finite; a program needn't handle non-finite values.
Results may differ from the reference program's by a relative error of at most 0.0057.
Values may be sent and summed in bfloat16 or wider, within the bound.
A program may use at most 128 MiB of HBM per device.

```python
import math
import jax
import jax.numpy as jnp
import numpy as np
from jax import lax

D = 7168
FF = 1024
TOK_DEV = 128
SECTIONS = 2
EXPERTS = 32
TOP = 8
CAP = 40
SLOTS = 1280
TOKENS = 4096


def levels(key, extent, cuts, least, top_value):
    def one(dim, blocks):
        steps = jax.random.uniform(jax.random.fold_in(jax.random.fold_in(key, 6), dim), (blocks,), jnp.float32, least / len(cuts), top_value / len(cuts))
        return jnp.repeat(jnp.exp(steps), extent[dim] // blocks).reshape((-1,) + (1,) * (len(extent) - dim - 1))

    gain = one(*cuts[0])
    for cut in cuts[1:]:
        gain = gain * one(*cut)
    return gain


def deal_out(own_key, own, number, rows, number_of, top, limit, lean):
    order = jax.random.permutation(own_key, number_of)
    heavy_load, usual = portions_of(number_of, rows * top, limit, lean, True), portions_of(number_of, rows * top, limit, lean, False)
    places = jnp.arange(number_of)

    def named(sizes, turn):
        used = int((sizes > 0).sum())
        fixed = max(1, used // 4)
        moved = fixed + (places - fixed + turn * (used - fixed)) % max(1, number_of - fixed)
        return jnp.zeros((number_of,), jnp.int32).at[order[jnp.where(places < fixed, places, moved)]].set(jnp.asarray(sizes, jnp.int32))

    sizes = jnp.where(number % 4 == 0, named(heavy_load, number // 4), named(usual, number - number // 4 - 1))
    mixed = jax.random.permutation(jax.random.fold_in(own, 3), number_of)
    source_of, receiver = mixed[0:number_of // 2 * 2:2], mixed[1:number_of // 2 * 2:2]
    slack = jnp.minimum(sizes[source_of] - 1, limit - sizes[receiver]) // 2
    slack = jnp.where((source_of == order[0]) | (receiver == order[0]) | (sizes[receiver] == 0), 0, jnp.maximum(slack, 0))
    moved = jax.random.randint(jax.random.fold_in(own, 4), (number_of // 2,), 0, 1 << 20) % (slack + 1)
    sizes = sizes.at[source_of].add(-moved).at[receiver].add(moved)
    members = jnp.searchsorted(jnp.cumsum(sizes), jnp.arange(rows * top), side="right").astype(jnp.int32)
    listing = members.reshape(top, rows).T
    listing = listing[jax.random.permutation(jax.random.fold_in(own, 1), rows)]
    turn = jax.random.randint(jax.random.fold_in(own, 2), (rows, 1), 0, top)
    return jnp.take_along_axis(listing, (jnp.arange(top)[None, :] + turn) % top, axis=1)


def portions_of(count, total, reach, skew, full):
    portions = [(1 << 20) // math.isqrt(grade ** skew) + 1 for grade in range(1, count + 1)]
    largest = reach if full else min(reach, max(-(-total // count), total * portions[0] // sum(portions)))
    least = 1 if total - largest >= count - 1 else 0
    given, surplus = [largest] + [least] * (count - 1), total - largest - least * (count - 1)
    while surplus > 0:
        movable = [i for i in range(1, count) if given[i] < largest] or [i for i in range(1, count) if given[i] < reach]
        pool, remaining = sum([portions[i] for i in movable]), surplus
        for i in movable:
            more = min(reach - given[i], max(1, remaining * portions[i] // pool), surplus)
            given[i] = given[i] + more
            surplus = surplus - more
    return np.array(given)


def centred(stream_key, extent, width, bound, cuts=(), kind=jnp.bfloat16):
    values = jax.random.normal(stream_key, extent, jnp.float32) * width
    if len(cuts) > 0:
        values = levels(stream_key, extent, cuts, -0.22, 0.18) * values
    return jnp.clip(values, min=-bound, max=bound).astype(kind)


def setup_inputs(seed: int = 0) -> dict:
    splits = jax.random.split(jax.random.key(seed), 9)
    out_grad = centred(splits[0], (SECTIONS, TOKENS, D), 1.0, 6.0, ((0, 2), (1, 32), (2, 4)))
    expert_ids_keys = jax.random.split(jax.random.fold_in(splits[1], 1), SECTIONS * TOKENS // TOK_DEV)
    expert_ids_turns = jax.random.permutation(jax.random.fold_in(splits[1], 3), SECTIONS * TOKENS // TOK_DEV)
    expert_ids = jax.vmap(lambda own, number: deal_out(jax.random.fold_in(splits[1], 2), own, number, TOK_DEV, EXPERTS, TOP, CAP, 1))(expert_ids_keys, expert_ids_turns).reshape((SECTIONS, TOKENS, TOP))
    gates = jnp.clip(0.05 + 0.55 * jax.random.uniform(splits[2], (SECTIONS, TOKENS, TOP), jnp.float32) ** levels(splits[2], (SECTIONS, TOKENS, TOP), ((0, 2), (1, 32)), -0.2, 0.2), 0.05, 0.6)
    w_gate = centred(splits[3], (SECTIONS, EXPERTS, D, FF), D ** -0.5, 0.0625, ((0, 2), (1, 32), (2, 4)))
    w_up = centred(splits[4], (SECTIONS, EXPERTS, D, FF), D ** -0.5, 0.0625, ((0, 2), (1, 32), (2, 4)))
    w_down = centred(splits[5], (SECTIONS, EXPERTS, FF, D), FF ** -0.5, 0.1875, ((0, 2), (1, 32), (3, 4)))
    gate_saved = centred(splits[6], (SECTIONS, EXPERTS, FF, SLOTS), 1.0, 4.0, ((0, 2), (1, 32), (2, 4)))
    up_saved = centred(splits[7], (SECTIONS, EXPERTS, FF, SLOTS), 1.0, 4.0, ((0, 2), (1, 32), (2, 4)))
    return dict(out_grad=out_grad, expert_ids=expert_ids, gates=gates, w_gate=w_gate, w_up=w_up, w_down=w_down, gate_saved=gate_saved, up_saved=up_saved)


def hidden_grads(hidden_sum, gate_part, up_part):
    pre = gate_part.astype(jnp.float32)
    upward = up_part.astype(jnp.float32)
    sigma = jax.nn.sigmoid(pre)
    up_grad = (hidden_sum * pre * sigma).astype(jnp.bfloat16)
    gate_grad = (hidden_sum * upward * sigma * (1.0 + pre * (1.0 - sigma))).astype(jnp.bfloat16)
    return (gate_grad, up_grad)

def section_grad(out_grad, routes, gates, w_gate, w_up, w_down, gate_saved, up_saved):
    count_rows = out_grad.shape[0]
    fanout = routes.shape[1]
    experts = w_down.shape[0]
    token_of = jnp.arange(count_rows, dtype=jnp.int32)
    source = token_of // TOK_DEV
    onehot = lax.optimization_barrier(jnp.sum((routes[:, :, None] == jnp.arange(experts, dtype=jnp.int32)).astype(jnp.int32), axis=1, dtype=jnp.int32))
    blocked = onehot.reshape(count_rows // TOK_DEV, TOK_DEV, experts)
    before = (jnp.cumsum(blocked, axis=1, dtype=jnp.int32) - blocked).reshape(count_rows, experts)
    position = jnp.take_along_axis(before, routes, axis=1).astype(jnp.int32)
    slot = (source[:, None] * CAP + position).astype(jnp.int32)
    owner_token = jnp.full((experts, SLOTS), -1, jnp.int32)
    owner_token = owner_token.at[routes.reshape(-1), slot.reshape(-1)].set(jnp.repeat(token_of, fanout))

    def expert_grad(packed):
        picked, gate_weight, up_weight, down_weight, gate_part, up_part = packed
        valid = picked >= 0
        rows = jnp.where(valid[:, None], out_grad[jnp.maximum(picked, 0)], jnp.zeros((), jnp.bfloat16))
        hidden_sum = jnp.dot(down_weight, rows.T, preferred_element_type=jnp.float32)
        gate_grad, up_grad = hidden_grads(hidden_sum, gate_part, up_part)
        total = jnp.dot(gate_grad.T, gate_weight.T, preferred_element_type=jnp.float32)
        total = total + jnp.dot(up_grad.T, up_weight.T, preferred_element_type=jnp.float32)
        return total.astype(jnp.bfloat16)
    slot_grads = lax.map(expert_grad, (owner_token, w_gate, w_up, w_down, gate_saved, up_saved))
    total = jnp.zeros(out_grad.shape, jnp.float32)
    for index in range(fanout):
        picked_rows = slot_grads[routes[:, index], slot[:, index]].astype(jnp.float32)
        total = total + gates[:, index][:, None] * picked_rows
    return total.astype(jnp.bfloat16)

def reference(out_grad, expert_ids, gates, w_gate, w_up, w_down, gate_saved, up_saved):
    results = []
    for section_index in range(SECTIONS):
        results.append(section_grad(out_grad[section_index], expert_ids[section_index], gates[section_index], w_gate[section_index], w_up[section_index], w_down[section_index], gate_saved[section_index], up_saved[section_index]))
    return jnp.stack([results[section_index ^ 1] for section_index in range(SECTIONS)])
```

```python
import jax
import jax.numpy as jnp
from jax import lax
from jax.experimental import pallas as pl
from jax.experimental.pallas import tpu as pltpu
from jax.sharding import PartitionSpec as P

MESH = pl.DeviceIdType.MESH
BF = jnp.bfloat16
F32 = jnp.float32
NX, NZ, NY = 4, 8, 4
TOK, W, FFL, CAP = 128, 1792, 256, 40
PAIR = 2 * CAP
CH = NX * PAIR
SLOTS = NX * NZ * CAP
PAIRS = ((0, 1), (-1, 2), (-2, 3), (-3, 4))
WHERE = {j: (c, h) for c, pair in enumerate(PAIRS) for h, j in enumerate(pair)}
NT = W // 256
WIRE = BF


def kernel(tokens, meta, wg, wu, wd, gsv, usv, out,
           tok, mt, sel, ghi, glo, xs, rows, hacc, part, hrecv, gu, ret, C, inp, inm, fin,
           gT, uT, gv, uv, wgv, wuv, wdv,
           agp_s, agp_r, agm_s, agm_r, mp_s, mp_r, mm_s, mm_r,
           xd_s, xd_r, yr_s, yr_r, yg_s, yg_r, xr_s, xr_r,
           rp_s, rp_r, rm_s, rm_r, f_s, f_r, loc):
    s = lax.axis_index("section")
    e = lax.axis_index("ep")
    y = lax.axis_index("tp")
    x = e // NZ
    z = lax.rem(e, NZ)

    def zdev(d):
        return (s, x * NZ + lax.rem(z + d + NZ, NZ), y)

    def xdev(o):
        return (s, lax.rem(x + o, NX) * NZ + z, y)

    def ydev(o):
        return (s, e, lax.rem(y + o, NY))

    partner = (1 - s, e, y)

    def remote(src, dst, ss, rs, dev):
        return pltpu.make_async_remote_copy(
            src_ref=src, dst_ref=dst, send_sem=ss, recv_sem=rs, device_id=dev, device_id_type=MESH)

    own_tok = pltpu.make_async_copy(tokens, tok.at[0, pl.ds(0, TOK)], loc.at[0])
    own_meta = pltpu.make_async_copy(meta, mt.at[0], loc.at[1])
    gcopy = pltpu.make_async_copy(gsv, gv, loc.at[2])
    ucopy = pltpu.make_async_copy(usv, uv, loc.at[3])
    dcopy = pltpu.make_async_copy(wd, wdv, loc.at[4])
    wgcopy = pltpu.make_async_copy(wg, wgv, loc.at[5])
    wucopy = pltpu.make_async_copy(wu, wuv, loc.at[6])
    for c in (own_tok, own_meta, gcopy, ucopy, dcopy, wgcopy, wucopy):
        c.start()

    barrier = pltpu.get_barrier_semaphore()
    peers = [zdev(1), zdev(-1)] + [xdev(o) for o in (1, 2, 3)] + [ydev(o) for o in (1, 2, 3)] + [partner]
    for dev in peers:
        pl.semaphore_signal(barrier, inc=1, device_id=dev, device_id_type=MESH)
    pl.semaphore_wait(barrier, len(peers))

    sends = []
    held = {}

    def begin(key, copy):
        copy.start()
        held[key] = copy
        sends.append(key)

    def arrived(key):
        held[key].wait_recv()

    def left(key):
        held[key].wait_send()
        sends.remove(key)

    def block(j, lo=0, n=TOK):
        c, h = WHERE[j]
        return tok.at[c, pl.ds(h * TOK + lo, n)]

    def metaof(j):
        c, h = WHERE[j]
        return mt.at[2 * c + h]

    half = TOK // 2

    def ag_send(d):
        k = d - 1
        if d < 4:
            begin(("ap", d), remote(block(k), block(d), agp_s.at[k], agp_r.at[k], zdev(-1)))
            begin(("am", d), remote(block(-k), block(-d), agm_s.at[k], agm_r.at[k], zdev(1)))
            begin(("mp", d), remote(metaof(k), metaof(d), mp_s.at[k], mp_r.at[k], zdev(-1)))
            begin(("mm", d), remote(metaof(-k), metaof(-d), mm_s.at[k], mm_r.at[k], zdev(1)))
        else:
            begin(("ap", d), remote(block(k, 0, half), block(4, 0, half), agp_s.at[k], agp_r.at[k], zdev(-1)))
            begin(("am", d), remote(block(-k, half, half), block(4, half, half), agm_s.at[k], agm_r.at[k], zdev(1)))
            begin(("mp", d), remote(metaof(k), metaof(4), mp_s.at[k], mp_r.at[k], zdev(-1)))

    def ag_wait(d):
        arrived(("mp", d))
        if d < 4:
            arrived(("mm", d))
        arrived(("ap", d))
        arrived(("am", d))

    def columns(n):
        return pl.ds(pl.multiple_of(n * 256, 256), 256)

    def select(c):
        t0 = lax.broadcasted_iota(jnp.int32, (TOK, TOK), 0)
        t1 = lax.broadcasted_iota(jnp.int32, (TOK, TOK), 1)
        earlier = (t0 < t1).astype(F32).astype(BF)
        rr = lax.broadcasted_iota(jnp.int32, (PAIR, 2 * TOK), 0)
        cc = lax.broadcasted_iota(jnp.int32, (PAIR, 2 * TOK), 1)
        same = (rr >= CAP) == (cc >= TOK)
        slot = jnp.where(rr >= CAP, rr - CAP, rr).astype(F32)
        r8 = lax.broadcasted_iota(jnp.int32, (8, TOK), 0)
        named, place, gate = [], [], []
        for h in range(2):
            ids = mt[2 * c + h, 0:8, :]
            gts = mt[2 * c + h, 8:16, :]
            m8 = jnp.zeros((8, TOK), F32)
            gs = []
            for o in range(NX):
                want = (lax.rem(x + o, NX) * NZ + z).astype(F32)
                hit = ids == want
                m = jnp.sum(hit.astype(F32), axis=0, keepdims=True)
                gs.append(jnp.sum(jnp.where(hit, gts, 0.0), axis=0, keepdims=True))
                m8 = jnp.where(r8 == o, m, m8)
            pos = jnp.dot(m8.astype(BF), earlier, preferred_element_type=F32)
            pos = jnp.where(m8 > 0.5, pos, -1.0)
            place.append(pos)
            gate.append(gs)
        for o in range(NX):
            pos2 = jnp.concatenate([place[0][o:o + 1], place[1][o:o + 1]], axis=1)
            g2 = jnp.concatenate([gate[0][o], gate[1][o]], axis=1)
            g_hi = g2.astype(BF).astype(F32)
            g_lo = g2 - g_hi
            hit = jnp.logical_and(slot == pos2, same)
            at = pl.ds(o * PAIR, PAIR)
            sel[c, at, :] = jnp.where(hit, 1.0, 0.0).astype(BF)
            ghi[c, at, :] = jnp.where(hit, g_hi, 0.0).astype(BF)
            glo[c, at, :] = jnp.where(hit, g_lo, 0.0).astype(BF)

        @pl.loop(0, NT)
        def _(n):
            got = jnp.dot(sel[c], tok[c, :, columns(n)], preferred_element_type=F32).astype(BF)
            rows[c, pl.ds(0, PAIR), columns(n)] = got[0:PAIR]
            xs[c, pl.ds(PAIR, 3 * PAIR), columns(n)] = got[PAIR:]

        for o in (2, 1, 3):
            begin(("xd", c, o), remote(xs.at[c, pl.ds(o * PAIR, PAIR)], rows.at[c, pl.ds((NX - o) * PAIR, PAIR)],
                                       xd_s.at[c, o - 1], xd_r.at[c, o - 1], xdev(o)))

    def first(c):
        for o in (1, 3, 2):
            arrived(("xd", c, o))
        for o in (1, 2, 3, 0):
            q = lax.rem(y + o, NY)
            acc = lax.dot_general(rows[c], wdv[columns(q), :], (((1,), (1,)), ((), ())), preferred_element_type=F32)
            if o:
                part[c, o - 1] = acc.astype(WIRE)
                begin(("yr", c, o), remote(part.at[c, o - 1], hrecv.at[c, o - 1], yr_s.at[c, o - 1], yr_r.at[c, o - 1], ydev(o)))
            else:
                hacc[c] = acc

    def grads(c):
        for o in (1, 2, 3):
            arrived(("yr", c, o))
        j1, j2 = PAIRS[c]
        for o in range(NX):
            at = pl.ds(o * PAIR, PAIR)
            h = hacc[c, at, :]
            for k in range(3):
                h = h + hrecv[c, k, at, :].astype(F32)
            base = lax.rem(x + o, NX) * NZ
            b1 = pl.ds(pl.multiple_of((base + lax.rem(z + j1 + NZ, NZ)) * CAP, 8), CAP)
            b2 = pl.ds(pl.multiple_of((base + lax.rem(z + j2 + NZ, NZ)) * CAP, 8), CAP)
            a = jnp.concatenate([gT[b1, :], gT[b2, :]], axis=0)
            u = jnp.concatenate([uT[b1, :], uT[b2, :]], axis=0)
            sigma = 1.0 / (1.0 + jnp.exp(-a))
            gu[c, y, 0, at, :] = (h * u * sigma * (1.0 + a * (1.0 - sigma))).astype(BF)
            gu[c, y, 1, at, :] = (h * a * sigma).astype(BF)
        for o in (2, 1, 3):
            begin(("yg", c, o), remote(gu.at[c, y], gu.at[c, y], yg_s.at[c, o - 1], yg_r.at[c, o - 1], ydev(o)))

    def second(c):
        for o in (1, 2, 3):
            left(("xd", c, o))
        for o in (1, 3, 2):
            src = lax.rem(y + NY - o, NY)
            remote(gu.at[c, src], gu.at[c, src], yg_s.at[c, o - 1], yg_r.at[c, o - 1], ydev(o)).wait_recv()

        @pl.loop(0, NT)
        def _(n):
            acc = jnp.zeros((CH, 256), F32)
            for q in range(NY):
                for i, w in ((0, wgv), (1, wuv)):
                    acc = acc + lax.dot_general(gu[c, q, i], w[columns(n), q * 256:(q + 1) * 256], (((1,), (1,)), ((), ())), preferred_element_type=F32)
            acc = acc.astype(BF)
            ret[c, pl.ds(0, PAIR), columns(n)] = acc[0:PAIR]
            xs[c, pl.ds(PAIR, 3 * PAIR), columns(n)] = acc[PAIR:]

    def give(c):
        for o in (2, 1, 3):
            begin(("xr", c, o), remote(xs.at[c, pl.ds(o * PAIR, PAIR)], ret.at[c, pl.ds((NX - o) * PAIR, PAIR)],
                                       xr_s.at[c, o - 1], xr_r.at[c, o - 1], xdev(o)))

    def combine(c):
        for o in (1, 3, 2):
            arrived(("xr", c, o))

        @pl.loop(0, NT)
        def _(n):
            r = ret[c, :, columns(n)]
            dims = (((0,), (0,)), ((), ()))
            C[c, :, columns(n)] = (lax.dot_general(ghi[c], r, dims, preferred_element_type=F32)
                                   + lax.dot_general(glo[c], r, dims, preferred_element_type=F32))

    def csum(j, lo, n, extra):
        c, h = WHERE[j]
        base = h * TOK + lo
        value = C[c, pl.ds(base, n), :]
        for r in extra:
            value = value + r.astype(F32)
        return value

    def chain(sign, j):
        inbox = inp if sign > 0 else inm
        ss, rs = (rp_s, rp_r) if sign > 0 else (rm_s, rm_r)
        name = "rp" if sign > 0 else "rm"
        dev = zdev(sign)
        lo = 0 if sign > 0 else half
        if j == 4:
            block(4, lo, half)[...] = csum(4, lo, half, ()).astype(BF)
            begin((name, j), remote(block(4, lo, half), inbox.at[3, pl.ds(lo, half)], ss.at[3], rs.at[3], dev))
            return
        arrived((name, j + 1))
        if j == 3:
            other = half - lo
            block(sign * j, lo, half)[...] = csum(sign * j, lo, half, (inbox[j, pl.ds(lo, half), :],)).astype(BF)
            block(sign * j, other, half)[...] = csum(sign * j, other, half, ()).astype(BF)
        else:
            block(sign * j)[...] = csum(sign * j, 0, TOK, (inbox[j],)).astype(BF)
        begin((name, j), remote(block(sign * j), inbox.at[j - 1], ss.at[j - 1], rs.at[j - 1], dev))

    own_tok.wait()
    own_meta.wait()
    ag_send(1)

    gcopy.wait()
    ucopy.wait()

    @pl.loop(0, SLOTS // 256)
    def _(i):
        gT[columns(i), :] = gv[:, columns(i)].astype(F32).T
        uT[columns(i), :] = uv[:, columns(i)].astype(F32).T

    ag_wait(1)
    ag_send(2)
    select(0)
    ag_wait(2)
    ag_send(3)
    select(1)
    dcopy.wait()
    first(0)
    ag_wait(3)
    ag_send(4)
    grads(0)
    ag_wait(4)
    select(3)
    select(2)
    for d in (1, 2, 3):
        for n in ("ap", "am", "mp", "mm"):
            left((n, d))
    for n in ("ap", "am", "mp"):
        left((n, 4))
    first(1)
    wgcopy.wait()
    wucopy.wait()
    second(0)
    grads(1)
    first(3)
    grads(3)
    second(1)
    first(2)
    give(0)
    give(1)
    grads(2)
    second(3)
    give(3)
    second(2)
    give(2)
    combine(0)
    combine(1)
    combine(3)
    chain(1, 4)
    chain(-1, 4)
    chain(-1, 3)
    combine(2)
    chain(1, 3)
    chain(-1, 2)
    chain(1, 2)
    chain(-1, 1)
    chain(1, 1)
    arrived(("rm", 1))
    arrived(("rp", 1))
    fin[...] = csum(0, 0, TOK, (inp[0], inm[0])).astype(BF)
    begin(("f",), remote(fin, out, f_s, f_r, partner))
    arrived(("f",))
    for key in list(sends):
        left(key)


def shards(out_grad, expert_ids, gates, w_gate, w_up, w_down, gate_saved, up_saved):
    meta = jnp.concatenate([expert_ids[0].T.astype(F32), gates[0].T], axis=0)
    dma = pltpu.SemaphoreType.DMA
    done = pl.pallas_call(
        kernel,
        out_shape=jax.ShapeDtypeStruct((TOK, W), BF),
        in_specs=[pl.BlockSpec(memory_space=pl.ANY)] * 7,
        out_specs=pl.BlockSpec(memory_space=pl.ANY),
        scratch_shapes=[
            pltpu.VMEM((4, 2 * TOK, W), BF),
            pltpu.VMEM((8, 16, TOK), F32),
            pltpu.VMEM((4, CH, 2 * TOK), BF),
            pltpu.VMEM((4, CH, 2 * TOK), BF),
            pltpu.VMEM((4, CH, 2 * TOK), BF),
            pltpu.VMEM((4, CH, W), BF),
            pltpu.VMEM((4, CH, W), BF),
            pltpu.VMEM((4, CH, FFL), F32),
            pltpu.VMEM((4, 3, CH, FFL), WIRE),
            pltpu.VMEM((4, 3, CH, FFL), WIRE),
            pltpu.VMEM((4, NY, 2, CH, FFL), BF),
            pltpu.VMEM((4, CH, W), BF),
            pltpu.VMEM((4, 2 * TOK, W), F32),
            pltpu.VMEM((4, TOK, W), BF),
            pltpu.VMEM((4, TOK, W), BF),
            pltpu.VMEM((TOK, W), BF),
            pltpu.VMEM((SLOTS, FFL), F32),
            pltpu.VMEM((SLOTS, FFL), F32),
            pltpu.VMEM((FFL, SLOTS), BF),
            pltpu.VMEM((FFL, SLOTS), BF),
            pltpu.VMEM((W, 1024), BF),
            pltpu.VMEM((W, 1024), BF),
            pltpu.VMEM((1024, W), BF),
        ] + [dma((4,))] * 8 + [dma((4, 3))] * 8 + [dma((4,))] * 4 + [dma, dma, dma((7,))],
        compiler_params=pltpu.CompilerParams(
            collective_id=0, has_side_effects=True, vmem_limit_bytes=63 * 2**20),
        cost_estimate=pl.CostEstimate(flops=16 * 10**9, bytes_accessed=14 * 10**6, transcendentals=3 * 10**5),
        name="expert_grad",
    )(out_grad[0], meta, w_gate[0, 0], w_up[0, 0], w_down[0, 0], gate_saved[0, 0], up_saved[0, 0])
    return done[None]


def solution(mesh):
    return jax.shard_map(
        shards,
        mesh=mesh,
        in_specs=(
            P("section", "ep", "tp"),
            P("section", "ep", None),
            P("section", "ep", None),
            P("section", "ep", "tp", None),
            P("section", "ep", "tp", None),
            P("section", "ep", None, "tp"),
            P("section", "ep", "tp", None),
            P("section", "ep", "tp", None),
        ),
        out_specs=P("section", "ep", "tp"),
        check_vma=False,
    )
```

```python
import jax
import jax.numpy as jnp
from jax import lax
from jax.experimental import pallas as pl
from jax.experimental.pallas import tpu as pltpu
from jax.sharding import PartitionSpec as P

MESH = pl.DeviceIdType.MESH
BF = jnp.bfloat16
F32 = jnp.float32
NX, NZ, NY = 4, 8, 4
TOK, W, FFL, CAP = 128, 1792, 256, 40
PAIR = 2 * CAP
CH = NX * PAIR
SLOTS = NX * NZ * CAP
PAIRS = ((0, 1), (-1, 2), (-2, 3), (-3, 4))
WHERE = {j: (c, h) for c, pair in enumerate(PAIRS) for h, j in enumerate(pair)}
NT = W // 256
WIRE = BF
POS = {1: 0, 3: 1, 0: 2, 2: 3}
GROUPS = ((1, 3), (0, 2))
HC = CH // 2
HALF = TOK // 2
PLAN = (
    ("ag", 1, 1), ("ag", 1, 0), ("ag", 2, 1), ("select", 0), ("send", 0, 1), ("ag", 2, 0), ("prepare",),
    ("ag", 3, 1), ("first", 0, 1), ("select", 1), ("send", 1, 1), ("send", 1, 0), ("ag", 3, 0), ("grads", 0, 1),
    ("ag", 4, 1), ("first", 1, 1), ("select", 2), ("ag", 4, 0), ("forward", 0, 1), ("send", 2, 0), ("grads", 1, 1),
    ("select", 3), ("first", 1, 0), ("send", 3, 1), ("send", 3, 0), ("first", 2, 0), ("send", 0, 0),
    ("second", 0, 1), ("forward", 1, 1), ("first", 3, 1), ("send", 2, 1), ("grads", 2, 0), ("grads", 3, 1),
    ("second", 1, 1), ("first", 3, 0), ("forward", 2, 0), ("give", 1, 1), ("forward", 3, 1), ("grads", 3, 0),
    ("first", 2, 1), ("second", 2, 0), ("give", 2, 0), ("second", 3, 1), ("give", 3, 1), ("forward", 3, 0),
    ("grads", 2, 1), ("second", 3, 0), ("forward", 2, 1), ("grads", 1, 0), ("first", 0, 0), ("give", 3, 0),
    ("second", 2, 1), ("forward", 1, 0), ("give", 2, 1), ("combine", 3), ("chain", 1, 4, 0), ("chain", -1, 4, 1),
    ("grads", 0, 0), ("second", 1, 0), ("give", 1, 0), ("chain", -1, 3, 0), ("combine", 2), ("chain", 1, 3, 1),
    ("forward", 0, 0), ("chain", -1, 3, 1), ("give", 0, 1), ("chain", 1, 3, 0), ("combine", 1), ("chain", -1, 2, 0),
    ("chain", 1, 2, 1), ("second", 0, 0), ("give", 0, 0), ("chain", -1, 2, 1), ("chain", 1, 2, 0), ("combine", 0),
    ("chain", -1, 1, 0), ("chain", 1, 1, 1), ("chain", -1, 1, 1), ("chain", 1, 1, 0), ("finish",),
)


def kernel(tokens, meta, wg, wu, wd, gsv, usv, out,
           tok, mt, sel, ghi, glo, xs, rows, hacc, part, hrecv, gu, ret, C, inp, inm, fin,
           gT, uT, gv, uv, wgv, wuv, wdv,
           ag_s, ag_r, rs_s, rs_r, m_s, m_r, xd_s, xd_r, xr_s, xr_r, yr_s, yr_r, yg_s, yg_r, f_s, f_r, loc):
    s = lax.axis_index("section")
    e = lax.axis_index("ep")
    y = lax.axis_index("tp")
    x = e // NZ
    z = lax.rem(e, NZ)

    def zdev(d):
        return (s, x * NZ + lax.rem(z + d + NZ, NZ), y)

    def xdev(o):
        return (s, lax.rem(x + o, NX) * NZ + z, y)

    def ydev(o):
        return (s, e, lax.rem(y + o, NY))

    partner = (1 - s, e, y)

    def remote(src, dst, ss, rs, dev):
        return pltpu.make_async_remote_copy(
            src_ref=src, dst_ref=dst, send_sem=ss, recv_sem=rs, device_id=dev, device_id_type=MESH)

    own_tok = pltpu.make_async_copy(tokens, tok.at[0, pl.ds(0, TOK)], loc.at[0])
    own_meta = pltpu.make_async_copy(meta, mt.at[0], loc.at[1])
    gcopy = pltpu.make_async_copy(gsv, gv, loc.at[2])
    ucopy = pltpu.make_async_copy(usv, uv, loc.at[3])
    dcopy = pltpu.make_async_copy(wd, wdv, loc.at[4])
    wgcopy = pltpu.make_async_copy(wg, wgv, loc.at[5])
    wucopy = pltpu.make_async_copy(wu, wuv, loc.at[6])
    locals_left = dict(tok=own_tok, meta=own_meta, gs=gcopy, us=ucopy, down=dcopy, wgate=wgcopy, wup=wucopy)
    for c in locals_left.values():
        c.start()

    def local(*names):
        for n in names:
            if n in locals_left:
                locals_left.pop(n).wait()

    barrier = pltpu.get_barrier_semaphore()
    peers = [zdev(1), zdev(-1)] + [xdev(o) for o in (1, 2, 3)] + [ydev(o) for o in (1, 2, 3)] + [partner]
    for dev in peers:
        pl.semaphore_signal(barrier, inc=1, device_id=dev, device_id_type=MESH)
    pl.semaphore_wait(barrier, len(peers))

    sends, pending, begun = {}, {}, set()

    def begin(key, copy, landing=None):
        copy.start()
        begun.add(key)
        sends[key] = copy
        pending[key] = landing or copy

    def arrived(key):
        if key in pending:
            pending.pop(key).wait_recv()

    def left(key):
        if key in sends:
            sends.pop(key).wait_send()

    def block(j, lo=0, n=TOK):
        c, h = WHERE[j]
        return tok.at[c, pl.ds(h * TOK + lo, n)]

    def metaof(j):
        c, h = WHERE[j]
        return mt.at[2 * c + h]

    def side(sign):
        return (1 - sign) // 2

    def ag(d, h):
        k = d - 1
        if d == 1:
            local("tok", "meta")
        for sign in ((1, -1) if d < 4 else ((1,), (-1,))[h]):
            i = side(sign)
            arrived(("a", k, sign, h))
            begin(("a", d, sign, h), remote(block(sign * k, h * HALF, HALF), block(d if d == 4 else sign * d, h * HALF, HALF),
                                            ag_s.at[i, k, h], ag_r.at[i, k, h], zdev(-sign)))
            if h == 0:
                arrived(("m", k, sign))
                begin(("m", d, sign), remote(metaof(sign * k), metaof(d if d == 4 else sign * d),
                                             m_s.at[i, k], m_r.at[i, k], zdev(-sign)))

    def columns(n):
        return pl.ds(pl.multiple_of(n * 256, 256), 256)

    def select(c):
        for j in PAIRS[c]:
            for sign in (1, -1) if j == 4 else (1,) if j > 0 else (-1,):
                arrived(("m", abs(j), sign))
                for h in range(2):
                    arrived(("a", abs(j), sign, h))
        t0 = lax.broadcasted_iota(jnp.int32, (TOK, TOK), 0)
        t1 = lax.broadcasted_iota(jnp.int32, (TOK, TOK), 1)
        earlier = (t0 < t1).astype(F32).astype(BF)
        rr = lax.broadcasted_iota(jnp.int32, (PAIR, 2 * TOK), 0)
        cc = lax.broadcasted_iota(jnp.int32, (PAIR, 2 * TOK), 1)
        same = (rr >= CAP) == (cc >= TOK)
        slot = jnp.where(rr >= CAP, rr - CAP, rr).astype(F32)
        r8 = lax.broadcasted_iota(jnp.int32, (8, TOK), 0)
        named, place, gate = [], [], []
        for h in range(2):
            ids = mt[2 * c + h, 0:8, :]
            gts = mt[2 * c + h, 8:16, :]
            m8 = jnp.zeros((8, TOK), F32)
            gs = []
            for o in range(NX):
                want = (lax.rem(x + o, NX) * NZ + z).astype(F32)
                hit = ids == want
                m = jnp.sum(hit.astype(F32), axis=0, keepdims=True)
                gs.append(jnp.sum(jnp.where(hit, gts, 0.0), axis=0, keepdims=True))
                m8 = jnp.where(r8 == o, m, m8)
            pos = jnp.dot(m8.astype(BF), earlier, preferred_element_type=F32)
            pos = jnp.where(m8 > 0.5, pos, -1.0)
            place.append(pos)
            gate.append(gs)
        for o in range(NX):
            pos2 = jnp.concatenate([place[0][o:o + 1], place[1][o:o + 1]], axis=1)
            g2 = jnp.concatenate([gate[0][o], gate[1][o]], axis=1)
            g_hi = g2.astype(BF).astype(F32)
            g_lo = g2 - g_hi
            hit = jnp.logical_and(slot == pos2, same)
            at = pl.ds(POS[o] * PAIR, PAIR)
            sel[c, at, :] = jnp.where(hit, 1.0, 0.0).astype(BF)
            ghi[c, at, :] = jnp.where(hit, g_hi, 0.0).astype(BF)
            glo[c, at, :] = jnp.where(hit, g_lo, 0.0).astype(BF)

        @pl.loop(0, NT, unroll=True)
        def _(n):
            got = jnp.dot(sel[c], tok[c, :, columns(n)], preferred_element_type=F32).astype(BF)
            xs[c, pl.ds(0, HC), columns(n)] = got[0:HC]
            rows[c, pl.ds(HC, PAIR), columns(n)] = got[HC:HC + PAIR]
            xs[c, pl.ds(HC + PAIR, PAIR), columns(n)] = got[HC + PAIR:]

    def across(name, c, g, dst, ss, rs):
        for o in GROUPS[g]:
            if o:
                begin((name, c, o), remote(xs.at[c, pl.ds(POS[o] * PAIR, PAIR)], dst.at[c, pl.ds(POS[NX - o] * PAIR, PAIR)],
                                           ss.at[c, o - 1], rs.at[c, o - 1], xdev(o)))

    def send(c, g):
        across("xd", c, g, rows, xd_s, xd_r)

    def give(c, g):
        across("xr", c, g, ret, xr_s, xr_r)

    def first(c, g):
        local("down")
        for o in GROUPS[g]:
            arrived(("xd", c, o))
        part_rows = pl.ds(g * HC, HC)
        for o in (2, 1, 3, 0):
            q = lax.rem(y + o, NY)
            acc = lax.dot_general(rows[c, part_rows, :], wdv[columns(q), :], (((1,), (1,)), ((), ())), preferred_element_type=F32)
            if o:
                part[c, g, o - 1] = acc.astype(WIRE)
                begin(("yr", c, g, o), remote(part.at[c, g, o - 1], hrecv.at[c, g, o - 1],
                                              yr_s.at[c, g, o - 1], yr_r.at[c, g, o - 1], ydev(o)))
            else:
                hacc[c, part_rows, :] = acc

    def grads(c, g):
        for o in (1, 2, 3):
            arrived(("yr", c, g, o))
        j1, j2 = PAIRS[c]
        for i, o in enumerate(GROUPS[g]):
            at = pl.ds(i * PAIR, PAIR)
            h = hacc[c, pl.ds(POS[o] * PAIR, PAIR), :]
            for k in range(3):
                h = h + hrecv[c, g, k, at, :].astype(F32)
            base = lax.rem(x + o, NX) * NZ
            b1 = pl.ds(pl.multiple_of((base + lax.rem(z + j1 + NZ, NZ)) * CAP, 8), CAP)
            b2 = pl.ds(pl.multiple_of((base + lax.rem(z + j2 + NZ, NZ)) * CAP, 8), CAP)
            a = jnp.concatenate([gT[b1, :], gT[b2, :]], axis=0)
            u = jnp.concatenate([uT[b1, :], uT[b2, :]], axis=0)
            sigma = 1.0 / (1.0 + jnp.exp(-a))
            gu[c, y, g, 0, at, :] = (h * u * sigma * (1.0 + a * (1.0 - sigma))).astype(BF)
            gu[c, y, g, 1, at, :] = (h * a * sigma).astype(BF)
        for k, step in enumerate((1, NY - 1)):
            swap(c, g, k, step, y, slice(None))

    def swap(c, g, k, step, holder, what):
        src = gu.at[c, holder, g] if what == slice(None) else gu.at[c, holder, g, what]
        origin = lax.rem(holder + NY - step, NY)
        landing = gu.at[c, origin, g] if what == slice(None) else gu.at[c, origin, g, what]
        ss, rs = yg_s.at[c, g, k], yg_r.at[c, g, k]
        begin(("yg", c, g, k), remote(src, src, ss, rs, ydev(step)), remote(landing, landing, ss, rs, ydev(step)))

    def forward(c, g):
        for k in range(2):
            arrived(("yg", c, g, k))
        for k, step in enumerate((1, NY - 1)):
            swap(c, g, 2 + k, step, lax.rem(y + NY - step, NY), k)

    def second(c, g):
        local("wgate", "wup")
        for o in GROUPS[g]:
            left(("xd", c, o))
        for k in range(4):
            arrived(("yg", c, g, k))

        @pl.loop(0, NT, unroll=True)
        def _(n):
            acc = jnp.zeros((HC, 256), F32)
            for q in range(NY):
                for i, w in ((0, wgv), (1, wuv)):
                    acc = acc + lax.dot_general(gu[c, q, g, i], w[columns(n), q * 256:(q + 1) * 256], (((1,), (1,)), ((), ())), preferred_element_type=F32)
            acc = acc.astype(BF)
            if g == 0:
                xs[c, pl.ds(0, HC), columns(n)] = acc
            else:
                ret[c, pl.ds(HC, PAIR), columns(n)] = acc[0:PAIR]
                xs[c, pl.ds(HC + PAIR, PAIR), columns(n)] = acc[PAIR:]

    def combine(c):
        for o in (1, 3, 2):
            arrived(("xr", c, o))

        @pl.loop(0, NT, unroll=True)
        def _(n):
            r = ret[c, :, columns(n)]
            dims = (((0,), (0,)), ((), ()))
            C[c, :, columns(n)] = (lax.dot_general(ghi[c], r, dims, preferred_element_type=F32)
                                   + lax.dot_general(glo[c], r, dims, preferred_element_type=F32))

    def csum(j, lo, n, extra):
        c, h = WHERE[j]
        base = h * TOK + lo
        value = C[c, pl.ds(base, n), :]
        for r in extra:
            value = value + r.astype(F32)
        return value

    def chain(sign, j, h):
        for key in list(sends):
            if key[0] == "a":
                left(key)
        inbox = inp if sign > 0 else inm
        i, lo = side(sign), h * HALF
        arrived(("r", sign, j + 1, h))
        extra = (inbox[j, pl.ds(lo, HALF), :],) if ("r", sign, j + 1, h) in begun else ()
        at = 4 if j == 4 else sign * j
        block(at, lo, HALF)[...] = csum(at, lo, HALF, extra).astype(BF)
        begin(("r", sign, j, h), remote(block(at, lo, HALF), inbox.at[j - 1, pl.ds(lo, HALF)],
                                        rs_s.at[i, j - 1, h], rs_r.at[i, j - 1, h], zdev(sign)))

    def prepare():
        local("gs", "us")

        @pl.loop(0, SLOTS // 256)
        def _(i):
            gT[columns(i), :] = gv[:, columns(i)].astype(F32).T
            uT[columns(i), :] = uv[:, columns(i)].astype(F32).T

    def finish():
        for h in range(2):
            for sign in (1, -1):
                arrived(("r", sign, 1, h))
            at = pl.ds(h * HALF, HALF)
            fin[at, :] = csum(0, h * HALF, HALF, (inp[0, at, :], inm[0, at, :])).astype(BF)
        begin(("f",), remote(fin, out, f_s, f_r, partner))
        arrived(("f",))

    verbs = dict(ag=ag, prepare=prepare, select=select, send=send, first=first, grads=grads, second=second, give=give,
                 forward=forward, combine=combine, chain=chain, finish=finish)
    for verb, *args in PLAN:
        verbs[verb](*args)
    for key in list(pending):
        arrived(key)
    for key in list(sends):
        left(key)


def shards(out_grad, expert_ids, gates, w_gate, w_up, w_down, gate_saved, up_saved):
    meta = jnp.concatenate([expert_ids[0].T.astype(F32), gates[0].T], axis=0)
    dma = pltpu.SemaphoreType.DMA
    done = pl.pallas_call(
        kernel,
        out_shape=jax.ShapeDtypeStruct((TOK, W), BF),
        in_specs=[pl.BlockSpec(memory_space=pl.ANY)] * 7,
        out_specs=pl.BlockSpec(memory_space=pl.ANY),
        scratch_shapes=[
            pltpu.VMEM((4, 2 * TOK, W), BF),
            pltpu.VMEM((8, 16, TOK), F32),
            pltpu.VMEM((4, CH, 2 * TOK), BF),
            pltpu.VMEM((4, CH, 2 * TOK), BF),
            pltpu.VMEM((4, CH, 2 * TOK), BF),
            pltpu.VMEM((4, CH, W), BF),
            pltpu.VMEM((4, CH, W), BF),
            pltpu.VMEM((4, CH, FFL), F32),
            pltpu.VMEM((4, 2, 3, HC, FFL), WIRE),
            pltpu.VMEM((4, 2, 3, HC, FFL), WIRE),
            pltpu.VMEM((4, NY, 2, 2, HC, FFL), BF),
            pltpu.VMEM((4, CH, W), BF),
            pltpu.VMEM((4, 2 * TOK, W), F32),
            pltpu.VMEM((4, TOK, W), BF),
            pltpu.VMEM((4, TOK, W), BF),
            pltpu.VMEM((TOK, W), BF),
            pltpu.VMEM((SLOTS, FFL), F32),
            pltpu.VMEM((SLOTS, FFL), F32),
            pltpu.VMEM((FFL, SLOTS), BF),
            pltpu.VMEM((FFL, SLOTS), BF),
            pltpu.VMEM((W, 1024), BF),
            pltpu.VMEM((W, 1024), BF),
            pltpu.VMEM((1024, W), BF),
        ] + [dma((2, 4, 2))] * 4 + [dma((2, 4))] * 2 + [dma((4, 3))] * 4 + [dma((4, 2, 3))] * 2 + [dma((4, 2, 4))] * 2 + [dma, dma, dma((7,))],
        compiler_params=pltpu.CompilerParams(
            collective_id=0, has_side_effects=True, vmem_limit_bytes=63 * 2**20),
        cost_estimate=pl.CostEstimate(flops=16 * 10**9, bytes_accessed=14 * 10**6, transcendentals=3 * 10**5),
        name="expert_grad",
    )(out_grad[0], meta, w_gate[0, 0], w_up[0, 0], w_down[0, 0], gate_saved[0, 0], up_saved[0, 0])
    return done[None]


def solution(mesh):
    return jax.shard_map(
        shards,
        mesh=mesh,
        in_specs=(
            P("section", "ep", "tp"),
            P("section", "ep", None),
            P("section", "ep", None),
            P("section", "ep", "tp", None),
            P("section", "ep", "tp", None),
            P("section", "ep", None, "tp"),
            P("section", "ep", "tp", None),
            P("section", "ep", "tp", None),
        ),
        out_specs=P("section", "ep", "tp"),
        check_vma=False,
    )
```

```python
import jax
import jax.numpy as jnp
from jax import lax
from jax.experimental import pallas as pl
from jax.experimental.pallas import tpu as pltpu
from jax.sharding import PartitionSpec as P

MESH = pl.DeviceIdType.MESH
BF = jnp.bfloat16
F32 = jnp.float32
NX, NZ, NY = 4, 8, 4
TOK, W, FFL, CAP = 128, 1792, 256, 40
PAIR = 2 * CAP
CH = NX * PAIR
SLOTS = NX * NZ * CAP
PAIRS = ((0, 1), (-1, 2), (-2, 3), (-3, 4))
WHERE = {j: (c, h) for c, pair in enumerate(PAIRS) for h, j in enumerate(pair)}
NT = W // 256
WIRE = BF
POS = {1: 0, 3: 1, 0: 2, 2: 3}
GROUPS = ((1, 3), (0, 2))
HC = CH // 2
HALF = TOK // 2
PLAN = (
    ("ag", 1, 1), ("ag", 1, 0), ("ag", 2, 1), ("select", 0), ("send", 0, 1), ("ag", 2, 0), ("prepare",),
    ("ag", 3, 1), ("first", 0, 1), ("select", 1), ("send", 1, 1), ("send", 1, 0), ("ag", 3, 0), ("grads", 0, 1),
    ("ag", 4, 1), ("first", 1, 1), ("select", 2), ("ag", 4, 0), ("forward", 0, 1), ("send", 2, 0), ("grads", 1, 1),
    ("select", 3), ("first", 1, 0), ("send", 3, 1), ("send", 3, 0), ("first", 2, 0), ("send", 0, 0),
    ("second", 0, 1), ("forward", 1, 1), ("first", 3, 1), ("send", 2, 1), ("grads", 2, 0), ("grads", 3, 1),
    ("second", 1, 1), ("first", 3, 0), ("forward", 2, 0), ("give", 1, 1), ("forward", 3, 1), ("grads", 3, 0),
    ("first", 2, 1), ("second", 2, 0), ("give", 2, 0), ("second", 3, 1), ("give", 3, 1), ("forward", 3, 0),
    ("grads", 2, 1), ("second", 3, 0), ("forward", 2, 1), ("grads", 1, 0), ("first", 0, 0), ("give", 3, 0),
    ("second", 2, 1), ("forward", 1, 0), ("give", 2, 1), ("combine", 3), ("chain", 1, 4, 0), ("chain", -1, 4, 1),
    ("grads", 0, 0), ("second", 1, 0), ("give", 1, 0), ("chain", -1, 3, 0), ("combine", 2), ("chain", 1, 3, 1),
    ("forward", 0, 0), ("chain", -1, 3, 1), ("give", 0, 1), ("chain", 1, 3, 0), ("combine", 1), ("chain", -1, 2, 0),
    ("chain", 1, 2, 1), ("second", 0, 0), ("give", 0, 0), ("chain", -1, 2, 1), ("chain", 1, 2, 0), ("combine", 0),
    ("chain", -1, 1, 0), ("chain", 1, 1, 1), ("chain", -1, 1, 1), ("chain", 1, 1, 0), ("finish",),
)


def kernel(tokens, ids_in, gates_in, wg, wu, wd, gsv, usv, out,
           tok, mt, sel, ghi, glo, xs, rows, hacc, part, hrecv, gu, ret, C, inp, inm, fin,
           gT, uT, gv, uv, wgv, wuv, wdv, idv, gtv,
           ag_s, ag_r, rs_s, rs_r, m_s, m_r, xd_s, xd_r, xr_s, xr_r, yr_s, yr_r, yg_s, yg_r, f_s, f_r, loc):
    s = lax.axis_index("section")
    e = lax.axis_index("ep")
    y = lax.axis_index("tp")
    x = e // NZ
    z = lax.rem(e, NZ)

    def zdev(d):
        return (s, x * NZ + lax.rem(z + d + NZ, NZ), y)

    def xdev(o):
        return (s, lax.rem(x + o, NX) * NZ + z, y)

    def ydev(o):
        return (s, e, lax.rem(y + o, NY))

    partner = (1 - s, e, y)

    def remote(src, dst, ss, rs, dev):
        return pltpu.make_async_remote_copy(
            src_ref=src, dst_ref=dst, send_sem=ss, recv_sem=rs, device_id=dev, device_id_type=MESH)

    own_tok = pltpu.make_async_copy(tokens, tok.at[0, pl.ds(0, TOK)], loc.at[0])
    own_ids = pltpu.make_async_copy(ids_in, idv, loc.at[1])
    own_gates = pltpu.make_async_copy(gates_in, gtv, loc.at[7])
    gcopy = pltpu.make_async_copy(gsv, gv, loc.at[2])
    ucopy = pltpu.make_async_copy(usv, uv, loc.at[3])
    dcopy = pltpu.make_async_copy(wd, wdv, loc.at[4])
    wgcopy = pltpu.make_async_copy(wg, wgv, loc.at[5])
    wucopy = pltpu.make_async_copy(wu, wuv, loc.at[6])
    locals_left = dict(tok=own_tok, ids=own_ids, gates=own_gates, gs=gcopy, us=ucopy, down=dcopy, wgate=wgcopy, wup=wucopy)
    for c in locals_left.values():
        c.start()

    def local(*names):
        for n in names:
            if n in locals_left:
                locals_left.pop(n).wait()

    barrier = pltpu.get_barrier_semaphore()
    peers = [zdev(1), zdev(-1)] + [xdev(o) for o in (1, 2, 3)] + [ydev(o) for o in (1, 2, 3)] + [partner]
    for dev in peers:
        pl.semaphore_signal(barrier, inc=1, device_id=dev, device_id_type=MESH)
    local("ids", "gates")
    mt[0, 0:8, :] = idv[...].astype(F32)
    mt[0, 8:16, :] = gtv[...]
    pl.semaphore_wait(barrier, len(peers))

    sends, pending, begun = {}, {}, set()

    def begin(key, copy, landing=None):
        copy.start()
        begun.add(key)
        sends[key] = copy
        pending[key] = landing or copy

    def arrived(key):
        if key in pending:
            pending.pop(key).wait_recv()

    def left(key):
        if key in sends:
            sends.pop(key).wait_send()

    def block(j, lo=0, n=TOK):
        c, h = WHERE[j]
        return tok.at[c, pl.ds(h * TOK + lo, n)]

    def metaof(j):
        c, h = WHERE[j]
        return mt.at[2 * c + h]

    def side(sign):
        return (1 - sign) // 2

    def ag(d, h):
        k = d - 1
        if d == 1:
            local("tok")
        for sign in ((1, -1) if d < 4 else ((1,), (-1,))[h]):
            i = side(sign)
            arrived(("a", k, sign, h))
            begin(("a", d, sign, h), remote(block(sign * k, h * HALF, HALF), block(d if d == 4 else sign * d, h * HALF, HALF),
                                            ag_s.at[i, k, h], ag_r.at[i, k, h], zdev(-sign)))
            if h == 0:
                arrived(("m", k, sign))
                begin(("m", d, sign), remote(metaof(sign * k), metaof(d if d == 4 else sign * d),
                                             m_s.at[i, k], m_r.at[i, k], zdev(-sign)))

    def columns(n):
        return pl.ds(pl.multiple_of(n * 256, 256), 256)

    def select(c):
        for j in PAIRS[c]:
            for sign in (1, -1) if j == 4 else (1,) if j > 0 else (-1,):
                arrived(("m", abs(j), sign))
                for h in range(2):
                    arrived(("a", abs(j), sign, h))
        t0 = lax.broadcasted_iota(jnp.int32, (TOK, TOK), 0)
        t1 = lax.broadcasted_iota(jnp.int32, (TOK, TOK), 1)
        earlier = (t0 < t1).astype(F32).astype(BF)
        rr = lax.broadcasted_iota(jnp.int32, (PAIR, 2 * TOK), 0)
        cc = lax.broadcasted_iota(jnp.int32, (PAIR, 2 * TOK), 1)
        same = (rr >= CAP) == (cc >= TOK)
        slot = jnp.where(rr >= CAP, rr - CAP, rr).astype(F32)
        r8 = lax.broadcasted_iota(jnp.int32, (8, TOK), 0)
        named, place, gate = [], [], []
        for h in range(2):
            ids = mt[2 * c + h, 0:8, :]
            gts = mt[2 * c + h, 8:16, :]
            m8 = jnp.zeros((8, TOK), F32)
            gs = []
            for o in range(NX):
                want = (lax.rem(x + o, NX) * NZ + z).astype(F32)
                hit = ids == want
                m = jnp.sum(hit.astype(F32), axis=0, keepdims=True)
                gs.append(jnp.sum(jnp.where(hit, gts, 0.0), axis=0, keepdims=True))
                m8 = jnp.where(r8 == o, m, m8)
            pos = jnp.dot(m8.astype(BF), earlier, preferred_element_type=F32)
            pos = jnp.where(m8 > 0.5, pos, -1.0)
            place.append(pos)
            gate.append(gs)
        for o in range(NX):
            pos2 = jnp.concatenate([place[0][o:o + 1], place[1][o:o + 1]], axis=1)
            g2 = jnp.concatenate([gate[0][o], gate[1][o]], axis=1)
            g_hi = g2.astype(BF).astype(F32)
            g_lo = g2 - g_hi
            hit = jnp.logical_and(slot == pos2, same)
            at = pl.ds(POS[o] * PAIR, PAIR)
            sel[c, at, :] = jnp.where(hit, 1.0, 0.0).astype(BF)
            ghi[c, at, :] = jnp.where(hit, g_hi, 0.0).astype(BF)
            glo[c, at, :] = jnp.where(hit, g_lo, 0.0).astype(BF)

        @pl.loop(0, NT, unroll=True)
        def _(n):
            got = jnp.dot(sel[c], tok[c, :, columns(n)], preferred_element_type=F32).astype(BF)
            xs[c, pl.ds(0, HC), columns(n)] = got[0:HC]
            rows[c, pl.ds(HC, PAIR), columns(n)] = got[HC:HC + PAIR]
            xs[c, pl.ds(HC + PAIR, PAIR), columns(n)] = got[HC + PAIR:]

    def across(name, c, g, dst, ss, rs):
        for o in GROUPS[g]:
            if o:
                begin((name, c, o), remote(xs.at[c, pl.ds(POS[o] * PAIR, PAIR)], dst.at[c, pl.ds(POS[NX - o] * PAIR, PAIR)],
                                           ss.at[c, o - 1], rs.at[c, o - 1], xdev(o)))

    def send(c, g):
        across("xd", c, g, rows, xd_s, xd_r)

    def give(c, g):
        across("xr", c, g, ret, xr_s, xr_r)

    def first(c, g):
        local("down")
        for o in GROUPS[g]:
            arrived(("xd", c, o))
        part_rows = pl.ds(g * HC, HC)
        for o in (2, 1, 3, 0):
            q = lax.rem(y + o, NY)
            acc = lax.dot_general(rows[c, part_rows, :], wdv[columns(q), :], (((1,), (1,)), ((), ())), preferred_element_type=F32)
            if o:
                part[c, g, o - 1] = acc.astype(WIRE)
                begin(("yr", c, g, o), remote(part.at[c, g, o - 1], hrecv.at[c, g, o - 1],
                                              yr_s.at[c, g, o - 1], yr_r.at[c, g, o - 1], ydev(o)))
            else:
                hacc[c, part_rows, :] = acc

    def grads(c, g):
        for o in (1, 2, 3):
            arrived(("yr", c, g, o))
        j1, j2 = PAIRS[c]
        for i, o in enumerate(GROUPS[g]):
            at = pl.ds(i * PAIR, PAIR)
            h = hacc[c, pl.ds(POS[o] * PAIR, PAIR), :]
            for k in range(3):
                h = h + hrecv[c, g, k, at, :].astype(F32)
            base = lax.rem(x + o, NX) * NZ
            b1 = pl.ds(pl.multiple_of((base + lax.rem(z + j1 + NZ, NZ)) * CAP, 8), CAP)
            b2 = pl.ds(pl.multiple_of((base + lax.rem(z + j2 + NZ, NZ)) * CAP, 8), CAP)
            a = jnp.concatenate([gT[b1, :], gT[b2, :]], axis=0)
            u = jnp.concatenate([uT[b1, :], uT[b2, :]], axis=0)
            sigma = 1.0 / (1.0 + jnp.exp(-a))
            gu[c, y, g, 0, at, :] = (h * u * sigma * (1.0 + a * (1.0 - sigma))).astype(BF)
            gu[c, y, g, 1, at, :] = (h * a * sigma).astype(BF)
        for k, step in enumerate((1, NY - 1)):
            swap(c, g, k, step, y, slice(None))

    def swap(c, g, k, step, holder, what):
        src = gu.at[c, holder, g] if what == slice(None) else gu.at[c, holder, g, what]
        origin = lax.rem(holder + NY - step, NY)
        landing = gu.at[c, origin, g] if what == slice(None) else gu.at[c, origin, g, what]
        ss, rs = yg_s.at[c, g, k], yg_r.at[c, g, k]
        begin(("yg", c, g, k), remote(src, src, ss, rs, ydev(step)), remote(landing, landing, ss, rs, ydev(step)))

    def forward(c, g):
        for k in range(2):
            arrived(("yg", c, g, k))
        for k, step in enumerate((1, NY - 1)):
            swap(c, g, 2 + k, step, lax.rem(y + NY - step, NY), k)

    def second(c, g):
        local("wgate", "wup")
        for o in GROUPS[g]:
            left(("xd", c, o))
        for k in range(4):
            arrived(("yg", c, g, k))

        @pl.loop(0, NT, unroll=True)
        def _(n):
            acc = jnp.zeros((HC, 256), F32)
            for q in range(NY):
                for i, w in ((0, wgv), (1, wuv)):
                    acc = acc + lax.dot_general(gu[c, q, g, i], w[columns(n), q * 256:(q + 1) * 256], (((1,), (1,)), ((), ())), preferred_element_type=F32)
            acc = acc.astype(BF)
            if g == 0:
                xs[c, pl.ds(0, HC), columns(n)] = acc
            else:
                ret[c, pl.ds(HC, PAIR), columns(n)] = acc[0:PAIR]
                xs[c, pl.ds(HC + PAIR, PAIR), columns(n)] = acc[PAIR:]

    def combine(c):
        for o in (1, 3, 2):
            arrived(("xr", c, o))

        @pl.loop(0, NT, unroll=True)
        def _(n):
            r = ret[c, :, columns(n)]
            dims = (((0,), (0,)), ((), ()))
            C[c, :, columns(n)] = (lax.dot_general(ghi[c], r, dims, preferred_element_type=F32)
                                   + lax.dot_general(glo[c], r, dims, preferred_element_type=F32))

    def csum(j, lo, n, extra):
        c, h = WHERE[j]
        base = h * TOK + lo
        value = C[c, pl.ds(base, n), :]
        for r in extra:
            value = value + r.astype(F32)
        return value

    def chain(sign, j, h):
        for key in list(sends):
            if key[0] == "a":
                left(key)
        inbox = inp if sign > 0 else inm
        i, lo = side(sign), h * HALF
        arrived(("r", sign, j + 1, h))
        extra = (inbox[j, pl.ds(lo, HALF), :],) if ("r", sign, j + 1, h) in begun else ()
        at = 4 if j == 4 else sign * j
        block(at, lo, HALF)[...] = csum(at, lo, HALF, extra).astype(BF)
        begin(("r", sign, j, h), remote(block(at, lo, HALF), inbox.at[j - 1, pl.ds(lo, HALF)],
                                        rs_s.at[i, j - 1, h], rs_r.at[i, j - 1, h], zdev(sign)))

    def prepare():
        local("gs", "us")

        @pl.loop(0, SLOTS // 256)
        def _(i):
            gT[columns(i), :] = gv[:, columns(i)].astype(F32).T
            uT[columns(i), :] = uv[:, columns(i)].astype(F32).T

    def finish():
        for h in range(2):
            for sign in (1, -1):
                arrived(("r", sign, 1, h))
            at = pl.ds(h * HALF, HALF)
            fin[at, :] = csum(0, h * HALF, HALF, (inp[0, at, :], inm[0, at, :])).astype(BF)
        begin(("f",), remote(fin, out, f_s, f_r, partner))
        arrived(("f",))

    verbs = dict(ag=ag, prepare=prepare, select=select, send=send, first=first, grads=grads, second=second, give=give,
                 forward=forward, combine=combine, chain=chain, finish=finish)
    for verb, *args in PLAN:
        verbs[verb](*args)
    for key in list(pending):
        arrived(key)
    for key in list(sends):
        left(key)


def shards(out_grad, expert_ids, gates, w_gate, w_up, w_down, gate_saved, up_saved):
    dma = pltpu.SemaphoreType.DMA
    done = pl.pallas_call(
        kernel,
        out_shape=jax.ShapeDtypeStruct((TOK, W), BF),
        in_specs=[pl.BlockSpec(memory_space=pl.ANY)] * 8,
        out_specs=pl.BlockSpec(memory_space=pl.ANY),
        scratch_shapes=[
            pltpu.VMEM((4, 2 * TOK, W), BF),
            pltpu.VMEM((8, 16, TOK), F32),
            pltpu.VMEM((4, CH, 2 * TOK), BF),
            pltpu.VMEM((4, CH, 2 * TOK), BF),
            pltpu.VMEM((4, CH, 2 * TOK), BF),
            pltpu.VMEM((4, CH, W), BF),
            pltpu.VMEM((4, CH, W), BF),
            pltpu.VMEM((4, CH, FFL), F32),
            pltpu.VMEM((4, 2, 3, HC, FFL), WIRE),
            pltpu.VMEM((4, 2, 3, HC, FFL), WIRE),
            pltpu.VMEM((4, NY, 2, 2, HC, FFL), BF),
            pltpu.VMEM((4, CH, W), BF),
            pltpu.VMEM((4, 2 * TOK, W), F32),
            pltpu.VMEM((4, TOK, W), BF),
            pltpu.VMEM((4, TOK, W), BF),
            pltpu.VMEM((TOK, W), BF),
            pltpu.VMEM((SLOTS, FFL), F32),
            pltpu.VMEM((SLOTS, FFL), F32),
            pltpu.VMEM((FFL, SLOTS), BF),
            pltpu.VMEM((FFL, SLOTS), BF),
            pltpu.VMEM((W, 1024), BF),
            pltpu.VMEM((W, 1024), BF),
            pltpu.VMEM((1024, W), BF),
            pltpu.VMEM((8, TOK), jnp.int32),
            pltpu.VMEM((8, TOK), F32),
        ] + [dma((2, 4, 2))] * 4 + [dma((2, 4))] * 2 + [dma((4, 3))] * 4 + [dma((4, 2, 3))] * 2 + [dma((4, 2, 4))] * 2 + [dma, dma, dma((8,))],
        compiler_params=pltpu.CompilerParams(
            collective_id=0, has_side_effects=True, vmem_limit_bytes=63 * 2**20),
        cost_estimate=pl.CostEstimate(flops=16 * 10**9, bytes_accessed=14 * 10**6, transcendentals=3 * 10**5),
        name="expert_grad",
    )(out_grad[0], expert_ids[0].T, gates[0].T, w_gate[0, 0], w_up[0, 0], w_down[0, 0], gate_saved[0, 0], up_saved[0, 0])
    return done[None]


def solution(mesh):
    return jax.shard_map(
        shards,
        mesh=mesh,
        in_specs=(
            P("section", "ep", "tp"),
            P("section", "ep", None),
            P("section", "ep", None),
            P("section", "ep", "tp", None),
            P("section", "ep", "tp", None),
            P("section", "ep", None, "tp"),
            P("section", "ep", "tp", None),
            P("section", "ep", "tp", None),
        ),
        out_specs=P("section", "ep", "tp"),
        check_vma=False,
    )
```

```python
import jax
import jax.numpy as jnp
from jax import lax
from jax.experimental import pallas as pl
from jax.experimental.pallas import tpu as pltpu
from jax.sharding import PartitionSpec as P

MESH = pl.DeviceIdType.MESH
BF = jnp.bfloat16
F32 = jnp.float32
NX, NZ, NY = 4, 8, 4
TOK, W, FFL, CAP = 128, 1792, 256, 40
PAIR = 2 * CAP
CH = NX * PAIR
SLOTS = NX * NZ * CAP
PAIRS = ((0, 1), (-1, 2), (-2, 3), (-3, 4))
WHERE = {j: (c, h) for c, pair in enumerate(PAIRS) for h, j in enumerate(pair)}
NT = W // 256
WIRE = BF
POS = {1: 0, 3: 1, 0: 2, 2: 3}
GROUPS = ((1, 3), (0, 2))
HC = CH // 2
HALF = TOK // 2
PLAN = (
    ("ag", 1, 0), ("prepare",), ("ag", 1, 1), ("ag", 2, 0), ("select", 0), ("send", 0, 0), ("ag", 2, 1),
    ("ag", 3, 0), ("select", 1), ("send", 1, 0), ("ag", 3, 1), ("first", 0, 0), ("send", 1, 1), ("grads", 0, 0),
    ("first", 1, 0), ("ag", 4, 0), ("ag", 4, 1), ("select", 2), ("send", 2, 0), ("first", 1, 1), ("select", 3),
    ("send", 3, 0), ("grads", 1, 0), ("first", 2, 0), ("send", 2, 1), ("forward", 1, 0), ("first", 3, 0),
    ("grads", 2, 0), ("send", 3, 1), ("second", 1, 0), ("grads", 3, 0), ("send", 0, 1), ("forward", 2, 0),
    ("give", 1, 0), ("first", 3, 1), ("forward", 3, 0), ("first", 2, 1), ("second", 2, 0), ("grads", 3, 1),
    ("second", 3, 0), ("give", 2, 0), ("grads", 2, 1), ("give", 3, 0), ("forward", 3, 1), ("grads", 1, 1),
    ("forward", 2, 1), ("first", 0, 1), ("second", 3, 1), ("give", 3, 1), ("forward", 1, 1), ("second", 2, 1),
    ("give", 2, 1), ("grads", 0, 1), ("combine", 3), ("forward", 0, 0), ("chain", 1, 4, 0), ("chain", -1, 4, 1),
    ("second", 1, 1), ("forward", 0, 1), ("give", 1, 1), ("chain", -1, 3, 0), ("combine", 2), ("chain", 1, 3, 1),
    ("second", 0, 0), ("give", 0, 0), ("chain", 1, 3, 0), ("chain", -1, 3, 1), ("second", 0, 1), ("give", 0, 1),
    ("chain", -1, 2, 0), ("combine", 1), ("chain", 1, 2, 1), ("chain", 1, 2, 0), ("chain", -1, 2, 1),
    ("chain", -1, 1, 0), ("combine", 0), ("chain", 1, 1, 1), ("chain", 1, 1, 0), ("chain", -1, 1, 1), ("finish",),
)


def kernel(tokens, ids_in, gates_in, wg, wu, wd, gsv, usv, out,
           tok, mt, sel, ghi, glo, xs, rows, hacc, part, hrecv, gu, ret, C, inp, inm, fin,
           gT, uT, gv, uv, wgv, wuv, wdv, idv, gtv,
           ag_s, ag_r, rs_s, rs_r, m_s, m_r, xd_s, xd_r, xr_s, xr_r, yr_s, yr_r, yg_s, yg_r, f_s, f_r, loc):
    s = lax.axis_index("section")
    e = lax.axis_index("ep")
    y = lax.axis_index("tp")
    x = e // NZ
    z = lax.rem(e, NZ)

    def zdev(d):
        return (s, x * NZ + lax.rem(z + d + NZ, NZ), y)

    def xdev(o):
        return (s, lax.rem(x + o, NX) * NZ + z, y)

    def ydev(o):
        return (s, e, lax.rem(y + o, NY))

    partner = (1 - s, e, y)

    def remote(src, dst, ss, rs, dev):
        return pltpu.make_async_remote_copy(
            src_ref=src, dst_ref=dst, send_sem=ss, recv_sem=rs, device_id=dev, device_id_type=MESH)

    own_tok = pltpu.make_async_copy(tokens, tok.at[0, pl.ds(0, TOK)], loc.at[0])
    own_ids = pltpu.make_async_copy(ids_in, idv, loc.at[1])
    own_gates = pltpu.make_async_copy(gates_in, gtv, loc.at[7])
    gcopy = pltpu.make_async_copy(gsv, gv, loc.at[2])
    ucopy = pltpu.make_async_copy(usv, uv, loc.at[3])
    dcopy = pltpu.make_async_copy(wd, wdv, loc.at[4])
    wgcopy = pltpu.make_async_copy(wg, wgv, loc.at[5])
    wucopy = pltpu.make_async_copy(wu, wuv, loc.at[6])
    locals_left = dict(tok=own_tok, ids=own_ids, gates=own_gates, gs=gcopy, us=ucopy, down=dcopy, wgate=wgcopy, wup=wucopy)
    for c in locals_left.values():
        c.start()

    def local(*names):
        for n in names:
            if n in locals_left:
                locals_left.pop(n).wait()

    barrier = pltpu.get_barrier_semaphore()
    peers = [zdev(1), zdev(-1)] + [xdev(o) for o in (1, 2, 3)] + [ydev(o) for o in (1, 2, 3)] + [partner]
    for dev in peers:
        pl.semaphore_signal(barrier, inc=1, device_id=dev, device_id_type=MESH)
    local("ids", "gates")
    mt[0, 0:8, :] = idv[...].astype(F32)
    mt[0, 8:16, :] = gtv[...]
    pl.semaphore_wait(barrier, len(peers))

    sends, pending, begun = {}, {}, set()

    def begin(key, copy, landing=None):
        copy.start()
        begun.add(key)
        sends[key] = copy
        pending[key] = landing or copy

    def arrived(key):
        if key in pending:
            pending.pop(key).wait_recv()

    def left(key):
        if key in sends:
            sends.pop(key).wait_send()

    def block(j, lo=0, n=TOK):
        c, h = WHERE[j]
        return tok.at[c, pl.ds(h * TOK + lo, n)]

    def metaof(j):
        c, h = WHERE[j]
        return mt.at[2 * c + h]

    def side(sign):
        return (1 - sign) // 2

    def ag(d, h):
        k = d - 1
        if d == 1:
            local("tok")
        for sign in ((1, -1) if d < 4 else ((1,), (-1,))[h]):
            i = side(sign)
            arrived(("a", k, sign, h))
            begin(("a", d, sign, h), remote(block(sign * k, h * HALF, HALF), block(d if d == 4 else sign * d, h * HALF, HALF),
                                            ag_s.at[i, k, h], ag_r.at[i, k, h], zdev(-sign)))
            if h == 0:
                arrived(("m", k, sign))
                begin(("m", d, sign), remote(metaof(sign * k), metaof(d if d == 4 else sign * d),
                                             m_s.at[i, k], m_r.at[i, k], zdev(-sign)))

    def columns(n):
        return pl.ds(pl.multiple_of(n * 256, 256), 256)

    def select(c):
        for j in PAIRS[c]:
            for sign in (1, -1) if j == 4 else (1,) if j > 0 else (-1,):
                arrived(("m", abs(j), sign))
                for h in range(2):
                    arrived(("a", abs(j), sign, h))
        t0 = lax.broadcasted_iota(jnp.int32, (TOK, TOK), 0)
        t1 = lax.broadcasted_iota(jnp.int32, (TOK, TOK), 1)
        earlier = (t0 < t1).astype(F32).astype(BF)
        rr = lax.broadcasted_iota(jnp.int32, (PAIR, 2 * TOK), 0)
        cc = lax.broadcasted_iota(jnp.int32, (PAIR, 2 * TOK), 1)
        same = (rr >= CAP) == (cc >= TOK)
        slot = jnp.where(rr >= CAP, rr - CAP, rr).astype(F32)
        r8 = lax.broadcasted_iota(jnp.int32, (8, TOK), 0)
        named, place, gate = [], [], []
        for h in range(2):
            ids = mt[2 * c + h, 0:8, :]
            gts = mt[2 * c + h, 8:16, :]
            m8 = jnp.zeros((8, TOK), F32)
            gs = []
            for o in range(NX):
                want = (lax.rem(x + o, NX) * NZ + z).astype(F32)
                hit = ids == want
                m = jnp.sum(hit.astype(F32), axis=0, keepdims=True)
                gs.append(jnp.sum(jnp.where(hit, gts, 0.0), axis=0, keepdims=True))
                m8 = jnp.where(r8 == o, m, m8)
            pos = jnp.dot(m8.astype(BF), earlier, preferred_element_type=F32)
            pos = jnp.where(m8 > 0.5, pos, -1.0)
            place.append(pos)
            gate.append(gs)
        for o in range(NX):
            pos2 = jnp.concatenate([place[0][o:o + 1], place[1][o:o + 1]], axis=1)
            g2 = jnp.concatenate([gate[0][o], gate[1][o]], axis=1)
            g_hi = g2.astype(BF).astype(F32)
            g_lo = g2 - g_hi
            hit = jnp.logical_and(slot == pos2, same)
            at = pl.ds(POS[o] * PAIR, PAIR)
            sel[c, at, :] = jnp.where(hit, 1.0, 0.0).astype(BF)
            ghi[c, at, :] = jnp.where(hit, g_hi, 0.0).astype(BF)
            glo[c, at, :] = jnp.where(hit, g_lo, 0.0).astype(BF)

        @pl.loop(0, NT, unroll=True)
        def _(n):
            got = jnp.dot(sel[c], tok[c, :, columns(n)], preferred_element_type=F32).astype(BF)
            xs[c, pl.ds(0, HC), columns(n)] = got[0:HC]
            rows[c, pl.ds(HC, PAIR), columns(n)] = got[HC:HC + PAIR]
            xs[c, pl.ds(HC + PAIR, PAIR), columns(n)] = got[HC + PAIR:]

    def across(name, c, g, dst, ss, rs):
        for o in GROUPS[g]:
            if o:
                begin((name, c, o), remote(xs.at[c, pl.ds(POS[o] * PAIR, PAIR)], dst.at[c, pl.ds(POS[NX - o] * PAIR, PAIR)],
                                           ss.at[c, o - 1], rs.at[c, o - 1], xdev(o)))

    def send(c, g):
        across("xd", c, g, rows, xd_s, xd_r)

    def give(c, g):
        across("xr", c, g, ret, xr_s, xr_r)

    def first(c, g):
        local("down")
        for o in GROUPS[g]:
            arrived(("xd", c, o))
        part_rows = pl.ds(g * HC, HC)
        for o in (2, 1, 3, 0):
            q = lax.rem(y + o, NY)
            acc = lax.dot_general(rows[c, part_rows, :], wdv[columns(q), :], (((1,), (1,)), ((), ())), preferred_element_type=F32)
            if o:
                part[c, g, o - 1] = acc.astype(WIRE)
                begin(("yr", c, g, o), remote(part.at[c, g, o - 1], hrecv.at[c, g, o - 1],
                                              yr_s.at[c, g, o - 1], yr_r.at[c, g, o - 1], ydev(o)))
            else:
                hacc[c, part_rows, :] = acc

    def grads(c, g):
        for o in (1, 2, 3):
            arrived(("yr", c, g, o))
        j1, j2 = PAIRS[c]
        for i, o in enumerate(GROUPS[g]):
            at = pl.ds(i * PAIR, PAIR)
            h = hacc[c, pl.ds(POS[o] * PAIR, PAIR), :]
            for k in range(3):
                h = h + hrecv[c, g, k, at, :].astype(F32)
            base = lax.rem(x + o, NX) * NZ
            b1 = pl.ds(pl.multiple_of((base + lax.rem(z + j1 + NZ, NZ)) * CAP, 8), CAP)
            b2 = pl.ds(pl.multiple_of((base + lax.rem(z + j2 + NZ, NZ)) * CAP, 8), CAP)
            a = jnp.concatenate([gT[b1, :], gT[b2, :]], axis=0)
            u = jnp.concatenate([uT[b1, :], uT[b2, :]], axis=0)
            sigma = 1.0 / (1.0 + jnp.exp(-a))
            gu[c, y, g, 0, at, :] = (h * u * sigma * (1.0 + a * (1.0 - sigma))).astype(BF)
            gu[c, y, g, 1, at, :] = (h * a * sigma).astype(BF)
        for k, step in enumerate((1, NY - 1)):
            swap(c, g, k, step, y, slice(None))

    def swap(c, g, k, step, holder, what):
        src = gu.at[c, holder, g] if what == slice(None) else gu.at[c, holder, g, what]
        origin = lax.rem(holder + NY - step, NY)
        landing = gu.at[c, origin, g] if what == slice(None) else gu.at[c, origin, g, what]
        ss, rs = yg_s.at[c, g, k], yg_r.at[c, g, k]
        begin(("yg", c, g, k), remote(src, src, ss, rs, ydev(step)), remote(landing, landing, ss, rs, ydev(step)))

    def forward(c, g):
        for k in range(2):
            arrived(("yg", c, g, k))
        for k, step in enumerate((1, NY - 1)):
            swap(c, g, 2 + k, step, lax.rem(y + NY - step, NY), k)

    def second(c, g):
        local("wgate", "wup")
        for o in GROUPS[g]:
            left(("xd", c, o))
        for k in range(4):
            arrived(("yg", c, g, k))

        @pl.loop(0, NT, unroll=True)
        def _(n):
            acc = jnp.zeros((HC, 256), F32)
            for q in range(NY):
                for i, w in ((0, wgv), (1, wuv)):
                    acc = acc + lax.dot_general(gu[c, q, g, i], w[columns(n), q * 256:(q + 1) * 256], (((1,), (1,)), ((), ())), preferred_element_type=F32)
            acc = acc.astype(BF)
            if g == 0:
                xs[c, pl.ds(0, HC), columns(n)] = acc
            else:
                ret[c, pl.ds(HC, PAIR), columns(n)] = acc[0:PAIR]
                xs[c, pl.ds(HC + PAIR, PAIR), columns(n)] = acc[PAIR:]

    def combine(c):
        for o in (1, 3, 2):
            arrived(("xr", c, o))

        @pl.loop(0, NT, unroll=True)
        def _(n):
            r = ret[c, :, columns(n)]
            dims = (((0,), (0,)), ((), ()))
            C[c, :, columns(n)] = (lax.dot_general(ghi[c], r, dims, preferred_element_type=F32)
                                   + lax.dot_general(glo[c], r, dims, preferred_element_type=F32))

    def csum(j, lo, n, extra):
        c, h = WHERE[j]
        base = h * TOK + lo
        value = C[c, pl.ds(base, n), :]
        for r in extra:
            value = value + r.astype(F32)
        return value

    def chain(sign, j, h):
        for key in list(sends):
            if key[0] == "a":
                left(key)
        inbox = inp if sign > 0 else inm
        i, lo = side(sign), h * HALF
        arrived(("r", sign, j + 1, h))
        extra = (inbox[j, pl.ds(lo, HALF), :],) if ("r", sign, j + 1, h) in begun else ()
        at = 4 if j == 4 else sign * j
        block(at, lo, HALF)[...] = csum(at, lo, HALF, extra).astype(BF)
        begin(("r", sign, j, h), remote(block(at, lo, HALF), inbox.at[j - 1, pl.ds(lo, HALF)],
                                        rs_s.at[i, j - 1, h], rs_r.at[i, j - 1, h], zdev(sign)))

    def prepare():
        local("gs", "us")

        @pl.loop(0, SLOTS // 256)
        def _(i):
            gT[columns(i), :] = gv[:, columns(i)].astype(F32).T
            uT[columns(i), :] = uv[:, columns(i)].astype(F32).T

    def finish():
        for h in range(2):
            for sign in (1, -1):
                arrived(("r", sign, 1, h))
            at = pl.ds(h * HALF, HALF)
            fin[at, :] = csum(0, h * HALF, HALF, (inp[0, at, :], inm[0, at, :])).astype(BF)
        begin(("f",), remote(fin, out, f_s, f_r, partner))
        arrived(("f",))

    verbs = dict(ag=ag, prepare=prepare, select=select, send=send, first=first, grads=grads, second=second, give=give,
                 forward=forward, combine=combine, chain=chain, finish=finish)
    for verb, *args in PLAN:
        verbs[verb](*args)
    for key in list(pending):
        arrived(key)
    for key in list(sends):
        left(key)


def shards(out_grad, expert_ids, gates, w_gate, w_up, w_down, gate_saved, up_saved):
    dma = pltpu.SemaphoreType.DMA
    done = pl.pallas_call(
        kernel,
        out_shape=jax.ShapeDtypeStruct((TOK, W), BF),
        in_specs=[pl.BlockSpec(memory_space=pl.ANY)] * 8,
        out_specs=pl.BlockSpec(memory_space=pl.ANY),
        scratch_shapes=[
            pltpu.VMEM((4, 2 * TOK, W), BF),
            pltpu.VMEM((8, 16, TOK), F32),
            pltpu.VMEM((4, CH, 2 * TOK), BF),
            pltpu.VMEM((4, CH, 2 * TOK), BF),
            pltpu.VMEM((4, CH, 2 * TOK), BF),
            pltpu.VMEM((4, CH, W), BF),
            pltpu.VMEM((4, CH, W), BF),
            pltpu.VMEM((4, CH, FFL), F32),
            pltpu.VMEM((4, 2, 3, HC, FFL), WIRE),
            pltpu.VMEM((4, 2, 3, HC, FFL), WIRE),
            pltpu.VMEM((4, NY, 2, 2, HC, FFL), BF),
            pltpu.VMEM((4, CH, W), BF),
            pltpu.VMEM((4, 2 * TOK, W), F32),
            pltpu.VMEM((4, TOK, W), BF),
            pltpu.VMEM((4, TOK, W), BF),
            pltpu.VMEM((TOK, W), BF),
            pltpu.VMEM((SLOTS, FFL), F32),
            pltpu.VMEM((SLOTS, FFL), F32),
            pltpu.VMEM((FFL, SLOTS), BF),
            pltpu.VMEM((FFL, SLOTS), BF),
            pltpu.VMEM((W, 1024), BF),
            pltpu.VMEM((W, 1024), BF),
            pltpu.VMEM((1024, W), BF),
            pltpu.VMEM((8, TOK), jnp.int32),
            pltpu.VMEM((8, TOK), F32),
        ] + [dma((2, 4, 2))] * 4 + [dma((2, 4))] * 2 + [dma((4, 3))] * 4 + [dma((4, 2, 3))] * 2 + [dma((4, 2, 4))] * 2 + [dma, dma, dma((8,))],
        compiler_params=pltpu.CompilerParams(
            collective_id=0, has_side_effects=True, vmem_limit_bytes=63 * 2**20),
        cost_estimate=pl.CostEstimate(flops=16 * 10**9, bytes_accessed=14 * 10**6, transcendentals=3 * 10**5),
        name="expert_grad",
    )(out_grad[0], expert_ids[0].T, gates[0].T, w_gate[0, 0], w_up[0, 0], w_down[0, 0], gate_saved[0, 0], up_saved[0, 0])
    return done[None]


def solution(mesh):
    return jax.shard_map(
        shards,
        mesh=mesh,
        in_specs=(
            P("section", "ep", "tp"),
            P("section", "ep", None),
            P("section", "ep", None),
            P("section", "ep", "tp", None),
            P("section", "ep", "tp", None),
            P("section", "ep", None, "tp"),
            P("section", "ep", "tp", None),
            P("section", "ep", "tp", None),
        ),
        out_specs=P("section", "ep", "tp"),
        check_vma=False,
    )
```
